32 devices in a mesh: section: 4 (over y, x), seq: 8 (over z, core).
Axes of the slice: x: 2, y: 2, z: 4, core: 2. Of those that a mesh axis runs over, the one named last changes fastest.
Arguments:
- tokens: bfloat16 [4, 2048, 4096], P('section', 'seq'), may hold values from -6 to 6
- norm_gain: bfloat16 [4, 4096], P('section'), may hold values from 0.099609375 to 1.8984375
- w_query: bfloat16 [4, 4096, 2048], P('section', 'seq'), may hold values from -0.09375 to 0.09375
- w_key: bfloat16 [4, 4096, 512], P('section', 'seq'), may hold values from -1.903125 to 1.903125
- w_value: bfloat16 [4, 4096, 512], P('section', 'seq'), may hold values from -0.09375 to 0.09375
Outputs:
- received: bfloat16 [4, 2048, 2048], P('section', 'seq')
The draws below stay inside these ranges and needn't reach their ends.
All inputs are finite; a program needn't handle non-finite values.
Results may differ from the reference program's by a relative error of at most 0.012.
The reference program's roundings to bfloat16 on the way count: a program that leaves them out, or rounds other values in their place, can miss the bound.
Values may be sent and summed in bfloat16 or wider, within the bound.
A program may use at most 192 MiB of HBM per device.

```python
import jax
import jax.numpy as jnp
from jax import lax

MODEL_WIDTH = 4096
LOCAL_QUERY_HEADS = 16
LOCAL_KEY_HEADS = 4
HEAD_SIZE = 128
SECTION_COUNT = 4
TOKENS = 2048
KW = 512


def paired_weights(key):
    query_portion = jax.random.normal(jax.random.fold_in(key, 101), (SECTION_COUNT, MODEL_WIDTH, LOCAL_QUERY_HEADS * HEAD_SIZE), jnp.float32)
    query_portion = jnp.clip(query_portion, -6.0, 6.0) * MODEL_WIDTH ** (-0.5)
    key_portion = jnp.clip(jax.random.normal(jax.random.fold_in(key, 104), (SECTION_COUNT, MODEL_WIDTH, LOCAL_KEY_HEADS * HEAD_SIZE), jnp.float32), -6.0, 6.0) * MODEL_WIDTH ** (-0.5)
    return (query_portion, key_portion)


def draw_w_query(key, part):
    return paired_weights(key)[0].astype(jnp.bfloat16)


def draw_w_key(key, part):
    return paired_weights(key)[1].astype(jnp.bfloat16)


def block_levels(key, extent, shards, low, top_value):
    def one(position, parts):
        heights = jax.random.uniform(jax.random.fold_in(jax.random.fold_in(key, 6), position), (parts,), jnp.float32, low / len(shards), top_value / len(shards))
        return jnp.repeat(jnp.exp(heights), extent[position] // parts).reshape((-1,) + (1,) * (len(extent) - position - 1))

    loudness = one(*shards[0])
    for cut in shards[1:]:
        loudness = loudness * one(*cut)
    return loudness


def centred(stream_key, shape, scale, limit, shards=(), dtype=jnp.bfloat16):
    values = jax.random.normal(stream_key, shape, jnp.float32) * scale
    if len(shards) > 0:
        values = block_levels(stream_key, shape, shards, -0.22, 0.18) * values
    return jnp.clip(values, min=-limit, max=limit).astype(dtype)


def setup_inputs(seed: int = 0) -> dict:
    keys = jax.random.split(jax.random.key(seed), 6)
    return {
        "tokens": centred(keys[0], (SECTION_COUNT, TOKENS, MODEL_WIDTH), 1.0, 6.0, ((0, 4), (1, 8))),
        "norm_gain": jnp.clip(1.0 + 0.18 * jax.random.normal(keys[1], (SECTION_COUNT, MODEL_WIDTH), jnp.float32), 0.099609375, 1.8984375).astype(jnp.bfloat16),
        "w_query": draw_w_query(jax.random.fold_in(keys[5], 71), 0),
        "w_key": draw_w_key(jax.random.fold_in(keys[5], 71), 0),
        "w_value": centred(keys[4], (SECTION_COUNT, MODEL_WIDTH, KW), MODEL_WIDTH ** -0.5, 0.09375, ((0, 4), (1, 8))),
    }


def normalize(rows_in, gain_row):
    wide = rows_in.astype(jnp.float32)
    scale = lax.rsqrt(lax.optimization_barrier(jnp.mean(wide * wide, axis=-1, keepdims=True)) + 1e-05)
    return (wide * scale * gain_row.astype(jnp.float32)).astype(jnp.bfloat16)

def rotate(matrix, positions):
    row_count = matrix.shape[0]
    head_count = matrix.shape[1] // HEAD_SIZE
    half_dim = HEAD_SIZE // 2
    shaped = matrix.reshape(row_count, head_count, HEAD_SIZE)
    freqs = jnp.power(jnp.float32(500000.0), -(jnp.arange(half_dim).astype(jnp.float32) * 2.0 / HEAD_SIZE))
    angles = positions[:, None] * freqs[None, :]
    cosine = jnp.cos(angles)[:, None, :]
    sine_part = jnp.sin(angles)[:, None, :]
    first_half = shaped[:, :, :half_dim]
    second_half = shaped[:, :, half_dim:]
    turned = jnp.concatenate([first_half * cosine - second_half * sine_part, second_half * cosine + first_half * sine_part], axis=2)
    return turned.reshape(row_count, head_count * HEAD_SIZE)

def expand(matrix):
    row_count = matrix.shape[0]
    kv_count = matrix.shape[1] // HEAD_SIZE
    query_group_count = LOCAL_QUERY_HEADS // LOCAL_KEY_HEADS
    wide = jnp.broadcast_to(matrix.reshape(row_count, kv_count, 1, HEAD_SIZE), (row_count, kv_count, query_group_count, HEAD_SIZE))
    return wide.reshape(row_count, kv_count * query_group_count * HEAD_SIZE)

def attend(queries, key_rows, value_rows):
    row_count = queries.shape[0]
    head_count = queries.shape[1] // HEAD_SIZE
    block_rows = min(512, row_count)
    key_heads = key_rows.reshape(row_count, head_count, HEAD_SIZE).astype(jnp.float32)
    value_heads = value_rows.reshape(row_count, head_count, HEAD_SIZE).astype(jnp.float32)
    key_places = jnp.arange(row_count).astype(jnp.int32)

    def one_block(block_index):
        first_row = (block_index * block_rows).astype(jnp.int32)
        query_block = lax.dynamic_slice_in_dim(queries, first_row, block_rows, 0)
        query_block = query_block.reshape(block_rows, head_count, HEAD_SIZE).astype(jnp.float32)
        scores = jnp.einsum('qhd,khd->hqk', query_block, key_heads, precision=lax.Precision.HIGHEST) / jnp.sqrt(jnp.float32(HEAD_SIZE))
        query_places = first_row + jnp.arange(block_rows).astype(jnp.int32)
        causal = key_places[None, :] <= query_places[:, None]
        scores = jnp.where(causal[None, :, :], scores, -jnp.inf)
        maxima = lax.optimization_barrier(jnp.max(scores, axis=-1, keepdims=True))
        expon = jnp.exp(scores - maxima)
        probs = (expon / lax.optimization_barrier(jnp.sum(expon, axis=-1, keepdims=True))).astype(jnp.bfloat16)
        mixed = jnp.einsum('hqk,khd->qhd', probs.astype(jnp.float32), value_heads, precision=lax.Precision.HIGHEST)
        return mixed.astype(jnp.bfloat16).reshape(block_rows, head_count * HEAD_SIZE)
    blocks = lax.map(one_block, jnp.arange(row_count // block_rows).astype(jnp.int32))
    return blocks.reshape(row_count, head_count * HEAD_SIZE)

def layer(operands):
    section_tokens, gain_row, query_weight, key_weight, value_weight = operands
    normed = normalize(section_tokens, gain_row)
    positions = jnp.arange(normed.shape[0]).astype(jnp.float32)
    queries = rotate(jnp.dot(normed, query_weight, preferred_element_type=jnp.float32), positions).astype(jnp.bfloat16)
    key_rows = rotate(jnp.dot(normed, key_weight, preferred_element_type=jnp.float32), positions).astype(jnp.bfloat16)
    value_rows = jnp.dot(normed, value_weight, preferred_element_type=jnp.float32).astype(jnp.bfloat16)
    return attend(queries, expand(key_rows), expand(value_rows))

def reference(tokens, norm_gain, w_query, w_key, w_value):
    outputs = lax.map(layer, (tokens, norm_gain, w_query, w_key, w_value))
    return jnp.roll(outputs, 1, axis=0)
```

```python
import functools

import jax
import jax.numpy as jnp
from jax import lax
from jax.experimental import pallas as pl
from jax.experimental.pallas import tpu as pltpu
from jax.sharding import PartitionSpec as P

HEAD = 128
LOG2E = 1.4426950408889634


def kernel(
    S, n, hq, group,
    tok_ref, gain_ref, wq_ref, wk_ref, wv_ref, cos_ref, sin_ref, out_ref,
    normed, xbuf, wqb, wkvb, qbuf, kvbuf, sbuf, obuf,
    xrecv, xsend, fsend, gsend, wqrecv, wqsend, wvrecv, wvsend, kvrecv, kvsend, orecv, osend,
):
    s = lax.axis_index("section")
    r = lax.axis_index("seq")
    p, c = r // 2, lax.rem(r, 2)
    v = 2 * s + c
    R = tok_ref.shape[0]
    T = xbuf.shape[0]
    K = xbuf.shape[1]
    piece = R // S
    kb = wq_ref.shape[0]
    qw = hq * HEAD
    prev = lax.rem(s + S - 1, S)
    nxt = lax.rem(p + 1, S)

    def dev(a, b):
        return {"section": a, "seq": b}

    def al(x, m):
        return pl.multiple_of(x, m)

    def post(src, dst, ssem, rsem, a, b):
        is_self = jnp.logical_and(a == s, b == r)

        @pl.when(is_self)
        def _():
            pltpu.make_async_copy(src, dst, rsem).start()

        @pl.when(jnp.logical_not(is_self))
        def _():
            pltpu.make_async_remote_copy(
                src_ref=src, dst_ref=dst, send_sem=ssem, recv_sem=rsem,
                device_id=dev(a, b), device_id_type=pl.DeviceIdType.MESH,
            ).start()

    def sent(src, ssem, a, b):
        @pl.when(jnp.logical_not(jnp.logical_and(a == s, b == r)))
        def _():
            pltpu.make_async_copy(src, src, ssem).wait()

    def arrived(ref, sem):
        pltpu.make_async_copy(ref, ref, sem).wait()

    barrier = pltpu.get_barrier_semaphore()

    def greet(a, b):
        pl.semaphore_signal(
            barrier, inc=1, device_id=dev(a, b), device_id_type=pl.DeviceIdType.MESH
        )

    for b in range(n):
        greet(p, jnp.int32(b))
    for a in range(S):
        for k in range(2):
            greet(jnp.int32(a), 2 * prev + k)
    for d in range(1, S):
        greet(lax.rem(s + d, S), r)
    greet(s, 2 * p + 1 - c)

    gain = gain_ref[...].astype(jnp.float32)

    def norm_step(i, _):
        rows = pl.ds(al(i * 32, 32), 32)
        wide = tok_ref[rows, :].astype(jnp.float32)
        scale = lax.rsqrt(jnp.mean(wide * wide, axis=-1, keepdims=True) + 1e-05)
        normed[rows, :] = (wide * scale * gain).astype(jnp.bfloat16)
        return 0

    lax.fori_loop(0, R // 32, norm_step, 0)
    pl.semaphore_wait(barrier, n + 2 * S + S)

    def xrows(seq, a):
        return xbuf.at[pl.ds(al(seq * R + a * piece, piece), piece), :]

    def first(d):
        a = lax.rem(s + d, S)
        return normed.at[pl.ds(al(a * piece, piece), piece), :], a

    for d in range(S):
        src, a = first(d)
        post(src, xrows(r, a), xsend.at[d], xrecv.at[r * S + a], a, 2 * s + c)

    def wparts(d, k):
        a = lax.rem(s + d, S)
        u = 2 * a + k
        qsrc = wq_ref.at[:, pl.ds(al(u * qw, 128), qw)]
        kvh = (u * hq) // group
        wsrc = (wk_ref, wv_ref)[k].at[:, pl.ds(al(kvh * HEAD, HEAD), HEAD)]
        return a, u, qsrc, wsrc

    krows = pl.ds(al(r * kb, kb), kb)
    for d in range(S):
        for k in range(2):
            a, u, qsrc, wsrc = wparts(d, k)
            post(qsrc, wqb.at[krows, :], wqsend.at[2 * d + k], wqrecv.at[r], a, 2 * s + k)
            post(wsrc, wkvb.at[krows, :], wvsend.at[2 * d + k], wvrecv.at[r], a, 2 * s + k)

    sib = 2 * p + 1 - c

    def relay(t, _):
        j = lax.rem(p + t, S)
        seq = 2 * j + c
        ref = xrows(seq, s)
        sem = xrecv.at[seq * S + s]
        arrived(ref, sem)
        for d in range(1, S):
            post(ref, ref, fsend.at[j * S + d - 1], sem, lax.rem(s + d, S), r)
        post(ref, ref, fsend.at[j * S + S - 1], sem, s, sib)
        return 0

    lax.fori_loop(0, S, relay, 0)

    def relay2(t, _):
        j = lax.rem(p + t, S)
        seq = 2 * j + c
        for d in range(1, S):
            a = lax.rem(s + d, S)
            ref = xrows(seq, a)
            sem = xrecv.at[seq * S + a]
            arrived(ref, sem)
            post(ref, ref, gsend.at[j * S + d - 1], sem, s, sib)
        return 0

    lax.fori_loop(0, S, relay2, 0)

    def gather_w(b, _):
        rows = pl.ds(al(b * kb, kb), kb)
        arrived(wqb.at[rows, :], wqrecv.at[b])
        arrived(wkvb.at[rows, :], wvrecv.at[b])
        return 0

    lax.fori_loop(0, n, gather_w, 0)

    is_k = c == 0

    def kvrows(slot, i):
        return kvbuf.at[slot, pl.ds(al(i * R, R), R), :]

    def project(t, _):
        j = lax.rem(p + t // 2, S)
        other = lax.rem(t, 2)
        i = 2 * j + lax.rem(c + other, 2)

        @pl.when(other == 1)
        def _():
            for a in range(S):
                arrived(xrows(i, a), xrecv.at[i * S + a])

        rows = pl.ds(al(i * R, R), R)
        x = xbuf[rows, :]
        co, si = cos_ref[rows, :], sin_ref[rows, :]
        q = jnp.dot(x, wqb[...], preferred_element_type=jnp.float32)
        for h in range(hq):
            qh = q[:, h * HEAD : (h + 1) * HEAD]
            qbuf[h, rows, :] = (qh * co + pltpu.roll(qh, HEAD // 2, 1) * si).astype(jnp.bfloat16)
        kv = jnp.dot(x, wkvb[...], preferred_element_type=jnp.float32)
        turned = kv * co + pltpu.roll(kv, HEAD // 2, 1) * si
        kvbuf[c, rows, :] = jnp.where(is_k, turned, kv).astype(jnp.bfloat16)
        post(kvrows(c, i), kvrows(c, i), kvsend.at[i], kvrecv.at[i], s, sib)
        return 0

    lax.fori_loop(0, n, project, 0)

    c2 = LOG2E / (HEAD**0.5)

    def oref(i):
        return obuf.at[i]

    ocols = pl.ds(al(v * qw, 128), qw)

    def attend(i, _):
        arrived(kvrows(1 - c, i), kvrecv.at[i])
        rows = pl.ds(al(i * R, R), R)
        for h in range(hq):
            qh = qbuf[h, rows, :]

            def score(t):
                kk = kvbuf[0, pl.ds(al(t * R, R), R), :]
                return lax.dot_general(
                    qh, kk, (((1,), (1,)), ((), ())), preferred_element_type=jnp.float32
                )

            def pass1(t, m):
                sc = score(t)
                sbuf[t] = sc
                return jnp.maximum(m, sc)

            sc = score(i)
            row = lax.broadcasted_iota(jnp.int32, (R, R), 0)
            col = lax.broadcasted_iota(jnp.int32, (R, R), 1)
            sc = jnp.where(col <= row, sc, -jnp.inf)
            sbuf[i] = sc
            m = lax.fori_loop(0, i, pass1, sc)
            top = jnp.max(m, axis=1, keepdims=True)

            def pass2(t, carry):
                acc, tot = carry
                e = jnp.exp2((sbuf[t] - top) * c2)
                vv = kvbuf[1, pl.ds(al(t * R, R), R), :]
                acc = acc + jnp.dot(
                    e.astype(jnp.bfloat16), vv, preferred_element_type=jnp.float32
                )
                return acc, tot + e

            acc, tot = lax.fori_loop(
                0, i + 1, pass2,
                (jnp.zeros((R, HEAD), jnp.float32), jnp.zeros((R, R), jnp.float32)),
            )
            total = jnp.sum(tot, axis=1, keepdims=True)
            obuf[i, :, h * HEAD : (h + 1) * HEAD] = (acc / total).astype(jnp.bfloat16)
        post(oref(i), out_ref.at[:, ocols], osend.at[i], orecv.at[v], nxt, i)
        return 0

    lax.fori_loop(0, n, attend, 0)

    for d in range(S):
        src, a = first(d)
        sent(src, xsend.at[d], a, 2 * s + c)
        for k in range(2):
            a, u, qsrc, wsrc = wparts(d, k)
            sent(wqb.at[krows, :], wqsend.at[2 * d + k], a, 2 * s + k)
            sent(wkvb.at[krows, :], wvsend.at[2 * d + k], a, 2 * s + k)

    def drain(j, _):
        ref = xrows(2 * j + c, s)
        for d in range(S):
            pltpu.make_async_copy(ref, ref, fsend.at[j * S + d]).wait()
        for d in range(1, S):
            o = xrows(2 * j + c, lax.rem(s + d, S))
            pltpu.make_async_copy(o, o, gsend.at[j * S + d - 1]).wait()
        return 0

    lax.fori_loop(0, S, drain, 0)

    def drain_out(i, _):
        pltpu.make_async_copy(kvrows(c, i), kvrows(c, i), kvsend.at[i]).wait()
        sent(oref(i), osend.at[i], nxt, i)
        o = out_ref.at[:, pl.ds(al(i * qw, 128), qw)]
        arrived(o, orecv.at[i])
        return 0

    lax.fori_loop(0, n, drain_out, 0)


def per_device(S, n, tokens, norm_gain, w_query, w_key, w_value):
    R, K = tokens.shape[1:]
    T = R * n
    heads = w_query.shape[2] // HEAD
    hq = heads // n
    group = heads // (w_key.shape[2] // HEAD)
    half = HEAD // 2
    freqs = jnp.power(
        jnp.float32(500000.0), -(jnp.arange(half).astype(jnp.float32) * 2.0 / HEAD)
    )
    angles = jnp.arange(T).astype(jnp.float32)[:, None] * freqs[None, :]
    cosine, sine = jnp.cos(angles), jnp.sin(angles)
    co = jnp.concatenate([cosine, cosine], axis=1)
    si = jnp.concatenate([-sine, sine], axis=1)
    vm = pl.BlockSpec(memory_space=pltpu.VMEM)
    hbm = pl.BlockSpec(memory_space=pl.ANY)
    dma = pltpu.SemaphoreType.DMA
    bf = jnp.bfloat16
    out = pl.pallas_call(
        functools.partial(kernel, S, n, hq, group),
        out_shape=jax.ShapeDtypeStruct((R, heads * HEAD), bf),
        in_specs=[vm, vm, hbm, hbm, hbm, vm, vm],
        out_specs=hbm,
        scratch_shapes=[
            pltpu.VMEM((R, K), bf),
            pltpu.VMEM((T, K), bf),
            pltpu.VMEM((K, hq * HEAD), bf),
            pltpu.VMEM((K, HEAD), bf),
            pltpu.VMEM((hq, T, HEAD), bf),
            pltpu.VMEM((2, T, HEAD), bf),
            pltpu.VMEM((n, R, R), jnp.float32),
            pltpu.VMEM((n, R, hq * HEAD), bf),
            dma((n * S,)), dma((S,)), dma((S * S,)), dma((S * S,)),
            dma((n,)), dma((n,)), dma((n,)), dma((n,)),
            dma((n,)), dma((n,)), dma((n,)), dma((n,)),
        ],
        compiler_params=pltpu.CompilerParams(
            collective_id=0, has_side_effects=True, vmem_limit_bytes=60 * 1024 * 1024
        ),
    )(tokens[0], norm_gain, w_query[0], w_key[0], w_value[0], co, si)
    return out[None]


def solution(mesh):
    S, n = mesh.shape["section"], mesh.shape["seq"]
    spec = P("section", "seq", None)
    return jax.shard_map(
        functools.partial(per_device, S, n),
        mesh=mesh,
        in_specs=(spec, P("section", None), spec, spec, spec),
        out_specs=spec,
        check_vma=False,
    )
```

```python
import functools

import jax
import jax.numpy as jnp
from jax import lax
from jax.experimental import pallas as pl
from jax.experimental.pallas import tpu as pltpu
from jax.sharding import PartitionSpec as P

HEAD = 128
LOG2E = 1.4426950408889634


def kernel(
    S, n, hq, group,
    tok_ref, gain_ref, wq_ref, wk_ref, wv_ref, cos_ref, sin_ref, out_ref,
    normed, xbuf, wqb, wkvb, qbuf, kvbuf, sbuf, obuf, xst, wsq, wsk, wsv,
    xsr, wsr, wss, xz, xrecv, xsend, fsend, gsend, wqrecv, wqsend, wvrecv, wvsend, kvrecv, kvsend, orecv, osend,
):
    s = lax.axis_index("section")
    r = lax.axis_index("seq")
    p, c = r // 2, lax.rem(r, 2)
    v = 2 * s + c
    R = tok_ref.shape[0]
    T = xbuf.shape[0]
    K = xbuf.shape[1]
    piece = R // S
    kb = wq_ref.shape[0]
    qw = hq * HEAD
    prev = lax.rem(s + S - 1, S)
    nxt = lax.rem(p + 1, S)

    def dev(a, b):
        return {"section": a, "seq": b}

    def al(x, m):
        return pl.multiple_of(x, m)

    def post(src, dst, ssem, rsem, a, b):
        is_self = jnp.logical_and(a == s, b == r)

        @pl.when(is_self)
        def _():
            pltpu.make_async_copy(src, dst, rsem).start()

        @pl.when(jnp.logical_not(is_self))
        def _():
            pltpu.make_async_remote_copy(
                src_ref=src, dst_ref=dst, send_sem=ssem, recv_sem=rsem,
                device_id=dev(a, b), device_id_type=pl.DeviceIdType.MESH,
            ).start()

    def sent(src, ssem, a, b):
        @pl.when(jnp.logical_not(jnp.logical_and(a == s, b == r)))
        def _():
            pltpu.make_async_copy(src, src, ssem).wait()

    def arrived(ref, sem):
        pltpu.make_async_copy(ref, ref, sem).wait()

    barrier = pltpu.get_barrier_semaphore()

    def greet(a, b):
        pl.semaphore_signal(
            barrier, inc=1, device_id=dev(a, b), device_id_type=pl.DeviceIdType.MESH
        )

    for b in range(n):
        greet(s, jnp.int32(b))
    for a in range(S):
        for k in range(2):
            greet(jnp.int32(a), 2 * prev + k)
    for d in range(S):
        greet(lax.rem(s + d, S), r)

    gain = gain_ref[...].astype(jnp.float32)

    def norm_step(i, _):
        rows = pl.ds(al(i * 32, 32), 32)
        wide = tok_ref[rows, :].astype(jnp.float32)
        scale = lax.rsqrt(jnp.mean(wide * wide, axis=-1, keepdims=True) + 1e-05)
        normed[rows, :] = (wide * scale * gain).astype(jnp.bfloat16)
        return 0

    lax.fori_loop(0, R // 32, norm_step, 0)
    pl.semaphore_wait(barrier, 2 * n + S)

    def xrows(seq, a):
        return xbuf.at[pl.ds(al(seq * R + a * piece, piece), piece), :]

    def first(d):
        a = lax.rem(s + d, S)
        return normed.at[pl.ds(al(a * piece, piece), piece), :], a

    for d in range(S):
        src, a = first(d)
        post(src, xst.at[s], xsend.at[d], xsr.at[s], a, r)

    def wfirst(d):
        a = lax.rem(s + d, S)
        head = pl.ds(al(((2 * a * hq) // group) * HEAD, HEAD), HEAD)
        return a, (
            (wq_ref.at[:, pl.ds(al(2 * a * qw, 128), 2 * qw)], wsq.at[s]),
            (wk_ref.at[:, head], wsk.at[s]),
            (wv_ref.at[:, head], wsv.at[s]),
        )

    for d in range(S):
        a, parts = wfirst(d)
        for k, (src, dst) in enumerate(parts):
            post(src, dst, wss.at[k, d], wsr.at[k, s], a, r)

    krows = pl.ds(al(r * kb, kb), kb)

    def second_x(t, _):
        j = lax.rem(p + 1 + t, S)
        arrived(xst.at[j], xsr.at[j])
        post(xst.at[j], xrows(r, s), xz.at[j], xrecv.at[r * S + s], s, 2 * j + c)
        return 0

    lax.fori_loop(0, S, second_x, 0)

    def second_w(t, _):
        j = lax.rem(p + 1 + t, S)
        for k, buf in enumerate((wsq, wsk, wsv)):
            arrived(buf.at[j], wsr.at[k, j])
        for k in range(2):
            post(
                wsq.at[j, :, k * qw : (k + 1) * qw], wqb.at[krows, :],
                wqsend.at[2 * j + k], wqrecv.at[r], s, 2 * j + k,
            )
            post(
                (wsk, wsv)[k].at[j], wkvb.at[krows, :],
                wvsend.at[2 * j + k], wvrecv.at[r], s, 2 * j + k,
            )
        return 0

    lax.fori_loop(0, S, second_w, 0)

    sib = 2 * p + 1 - c

    def relay(t, _):
        j = lax.rem(p + t, S)
        seq = 2 * j + c
        ref = xrows(seq, s)
        sem = xrecv.at[seq * S + s]
        arrived(ref, sem)
        for d in range(1, S):
            post(ref, ref, fsend.at[j * S + d - 1], sem, lax.rem(s + d, S), r)
        post(ref, ref, fsend.at[j * S + S - 1], sem, s, sib)
        return 0

    lax.fori_loop(0, S, relay, 0)

    def relay2(t, _):
        j = lax.rem(p + t, S)
        seq = 2 * j + c
        for d in range(1, S):
            a = lax.rem(s + d, S)
            ref = xrows(seq, a)
            sem = xrecv.at[seq * S + a]
            arrived(ref, sem)
            post(ref, ref, gsend.at[j * S + d - 1], sem, s, sib)
        return 0

    lax.fori_loop(0, S, relay2, 0)

    def gather_w(b, _):
        rows = pl.ds(al(b * kb, kb), kb)
        arrived(wqb.at[rows, :], wqrecv.at[b])
        arrived(wkvb.at[rows, :], wvrecv.at[b])
        return 0

    lax.fori_loop(0, n, gather_w, 0)

    is_k = c == 0

    def kvrows(slot, i):
        return kvbuf.at[slot, pl.ds(al(i * R, R), R), :]

    def project(t, _):
        j = lax.rem(p + t // 2, S)
        other = lax.rem(t, 2)
        i = 2 * j + lax.rem(c + other, 2)

        @pl.when(other == 1)
        def _():
            for a in range(S):
                arrived(xrows(i, a), xrecv.at[i * S + a])

        rows = pl.ds(al(i * R, R), R)
        x = xbuf[rows, :]
        co, si = cos_ref[rows, :], sin_ref[rows, :]
        q = jnp.dot(x, wqb[...], preferred_element_type=jnp.float32)
        for h in range(hq):
            qh = q[:, h * HEAD : (h + 1) * HEAD]
            qbuf[h, rows, :] = (qh * co + pltpu.roll(qh, HEAD // 2, 1) * si).astype(jnp.bfloat16)
        kv = jnp.dot(x, wkvb[...], preferred_element_type=jnp.float32)
        turned = kv * co + pltpu.roll(kv, HEAD // 2, 1) * si
        kvbuf[c, rows, :] = jnp.where(is_k, turned, kv).astype(jnp.bfloat16)
        post(kvrows(c, i), kvrows(c, i), kvsend.at[i], kvrecv.at[i], s, sib)
        return 0

    lax.fori_loop(0, n, project, 0)

    c2 = LOG2E / (HEAD**0.5)

    def oref(i):
        return obuf.at[i]

    ocols = pl.ds(al(v * qw, 128), qw)

    def attend(i, _):
        arrived(kvrows(1 - c, i), kvrecv.at[i])
        rows = pl.ds(al(i * R, R), R)
        for h in range(hq):
            qh = qbuf[h, rows, :]

            def score(t):
                kk = kvbuf[0, pl.ds(al(t * R, R), R), :]
                return lax.dot_general(
                    qh, kk, (((1,), (1,)), ((), ())), preferred_element_type=jnp.float32
                )

            def pass1(t, m):
                sc = score(t)
                sbuf[t] = sc
                return jnp.maximum(m, sc)

            sc = score(i)
            row = lax.broadcasted_iota(jnp.int32, (R, R), 0)
            col = lax.broadcasted_iota(jnp.int32, (R, R), 1)
            sc = jnp.where(col <= row, sc, -jnp.inf)
            sbuf[i] = sc
            m = lax.fori_loop(0, i, pass1, sc)
            top = jnp.max(m, axis=1, keepdims=True)

            def pass2(t, carry):
                acc, tot = carry
                e = jnp.exp2((sbuf[t] - top) * c2)
                vv = kvbuf[1, pl.ds(al(t * R, R), R), :]
                acc = acc + jnp.dot(
                    e.astype(jnp.bfloat16), vv, preferred_element_type=jnp.float32
                )
                return acc, tot + e

            acc, tot = lax.fori_loop(
                0, i + 1, pass2,
                (jnp.zeros((R, HEAD), jnp.float32), jnp.zeros((R, R), jnp.float32)),
            )
            total = jnp.sum(tot, axis=1, keepdims=True)
            obuf[i, :, h * HEAD : (h + 1) * HEAD] = (acc / total).astype(jnp.bfloat16)
        post(oref(i), out_ref.at[:, ocols], osend.at[i], orecv.at[v], nxt, i)
        return 0

    lax.fori_loop(0, n, attend, 0)

    for d in range(S):
        src, a = first(d)
        sent(src, xsend.at[d], a, r)
        a, parts = wfirst(d)
        for k, (_, dst) in enumerate(parts):
            sent(dst, wss.at[k, d], a, r)

    def drain(j, _):
        sent(xst.at[j], xz.at[j], s, 2 * j + c)
        for k in range(2):
            sent(wqb.at[krows, :], wqsend.at[2 * j + k], s, 2 * j + k)
            sent(wkvb.at[krows, :], wvsend.at[2 * j + k], s, 2 * j + k)
        ref = xrows(2 * j + c, s)
        for d in range(S):
            pltpu.make_async_copy(ref, ref, fsend.at[j * S + d]).wait()
        for d in range(1, S):
            o = xrows(2 * j + c, lax.rem(s + d, S))
            pltpu.make_async_copy(o, o, gsend.at[j * S + d - 1]).wait()
        return 0

    lax.fori_loop(0, S, drain, 0)

    def drain_out(i, _):
        pltpu.make_async_copy(kvrows(c, i), kvrows(c, i), kvsend.at[i]).wait()
        sent(oref(i), osend.at[i], nxt, i)
        o = out_ref.at[:, pl.ds(al(i * qw, 128), qw)]
        arrived(o, orecv.at[i])
        return 0

    lax.fori_loop(0, n, drain_out, 0)


def per_device(S, n, tokens, norm_gain, w_query, w_key, w_value):
    R, K = tokens.shape[1:]
    T = R * n
    heads = w_query.shape[2] // HEAD
    hq = heads // n
    group = heads // (w_key.shape[2] // HEAD)
    half = HEAD // 2
    freqs = jnp.power(
        jnp.float32(500000.0), -(jnp.arange(half).astype(jnp.float32) * 2.0 / HEAD)
    )
    angles = jnp.arange(T).astype(jnp.float32)[:, None] * freqs[None, :]
    cosine, sine = jnp.cos(angles), jnp.sin(angles)
    co = jnp.concatenate([cosine, cosine], axis=1)
    si = jnp.concatenate([-sine, sine], axis=1)
    vm = pl.BlockSpec(memory_space=pltpu.VMEM)
    hbm = pl.BlockSpec(memory_space=pl.ANY)
    dma = pltpu.SemaphoreType.DMA
    bf = jnp.bfloat16
    out = pl.pallas_call(
        functools.partial(kernel, S, n, hq, group),
        out_shape=jax.ShapeDtypeStruct((R, heads * HEAD), bf),
        in_specs=[vm, vm, hbm, hbm, hbm, vm, vm],
        out_specs=hbm,
        scratch_shapes=[
            pltpu.VMEM((R, K), bf),
            pltpu.VMEM((T, K), bf),
            pltpu.VMEM((K, hq * HEAD), bf),
            pltpu.VMEM((K, HEAD), bf),
            pltpu.VMEM((hq, T, HEAD), bf),
            pltpu.VMEM((2, T, HEAD), bf),
            pltpu.VMEM((n, R, R), jnp.float32),
            pltpu.VMEM((n, R, hq * HEAD), bf),
            pltpu.VMEM((S, R // S, K), bf),
            pltpu.VMEM((S, K // n, 2 * hq * HEAD), bf),
            pltpu.VMEM((S, K // n, HEAD), bf),
            pltpu.VMEM((S, K // n, HEAD), bf),
            dma((S,)), dma((3, S)), dma((3, S)), dma((S,)),
            dma((n * S,)), dma((S,)), dma((S * S,)), dma((S * S,)),
            dma((n,)), dma((n,)), dma((n,)), dma((n,)),
            dma((n,)), dma((n,)), dma((n,)), dma((n,)),
        ],
        compiler_params=pltpu.CompilerParams(
            collective_id=0, has_side_effects=True, vmem_limit_bytes=60 * 1024 * 1024
        ),
    )(tokens[0], norm_gain, w_query[0], w_key[0], w_value[0], co, si)
    return out[None]


def solution(mesh):
    S, n = mesh.shape["section"], mesh.shape["seq"]
    spec = P("section", "seq", None)
    return jax.shard_map(
        functools.partial(per_device, S, n),
        mesh=mesh,
        in_specs=(spec, P("section", None), spec, spec, spec),
        out_specs=spec,
        check_vma=False,
    )
```

```python
import functools

import jax
import jax.numpy as jnp
from jax import lax
from jax.experimental import pallas as pl
from jax.experimental.pallas import tpu as pltpu
from jax.sharding import PartitionSpec as P

HEAD = 128
LOG2E = 1.4426950408889634


def kernel(
    S, n, hq, group,
    tok_ref, gain_ref, wq_ref, wk_ref, wv_ref, cos_ref, sin_ref, out_ref,
    normed, xbuf, wqb, wkvb, qbuf, kvbuf, sbuf, obuf, xst, wsq, wsk, wsv,
    xsr, wsr, wss, xz, xrecv, xsend, fsend, gsend, wqrecv, wqsend, wvrecv, wvsend, kvrecv, kvsend, orecv, osend,
):
    s = lax.axis_index("section")
    r = lax.axis_index("seq")
    p, c = r // 2, lax.rem(r, 2)
    v = 2 * s + c
    R = tok_ref.shape[0]
    T = xbuf.shape[0]
    K = xbuf.shape[1]
    piece = R // S
    kb = wq_ref.shape[0]
    qw = hq * HEAD
    prev = lax.rem(s + S - 1, S)
    nxt = lax.rem(p + 1, S)

    def dev(a, b):
        return {"section": a, "seq": b}

    def al(x, m):
        return pl.multiple_of(x, m)

    def post(src, dst, ssem, rsem, a, b):
        is_self = jnp.logical_and(a == s, b == r)

        @pl.when(is_self)
        def _():
            pltpu.make_async_copy(src, dst, rsem).start()

        @pl.when(jnp.logical_not(is_self))
        def _():
            pltpu.make_async_remote_copy(
                src_ref=src, dst_ref=dst, send_sem=ssem, recv_sem=rsem,
                device_id=dev(a, b), device_id_type=pl.DeviceIdType.MESH,
            ).start()

    def sent(src, ssem, a, b):
        @pl.when(jnp.logical_not(jnp.logical_and(a == s, b == r)))
        def _():
            pltpu.make_async_copy(src, src, ssem).wait()

    def arrived(ref, sem):
        pltpu.make_async_copy(ref, ref, sem).wait()

    barrier = pltpu.get_barrier_semaphore()

    def greet(a, b):
        pl.semaphore_signal(
            barrier, inc=1, device_id=dev(a, b), device_id_type=pl.DeviceIdType.MESH
        )

    for b in range(n):
        greet(s, jnp.int32(b))
    for a in range(S):
        for k in range(2):
            greet(jnp.int32(a), 2 * prev + k)
    for d in range(S):
        greet(lax.rem(s + d, S), r)

    gain = gain_ref[...].astype(jnp.float32)

    def norm_step(i, _):
        rows = pl.ds(al(i * 32, 32), 32)
        wide = tok_ref[rows, :].astype(jnp.float32)
        scale = lax.rsqrt(jnp.mean(wide * wide, axis=-1, keepdims=True) + 1e-05)
        normed[rows, :] = (wide * scale * gain).astype(jnp.bfloat16)
        return 0

    lax.fori_loop(0, R // 32, norm_step, 0)
    pl.semaphore_wait(barrier, 2 * n + S)

    def xrows(seq, a):
        return xbuf.at[pl.ds(al(seq * R + a * piece, piece), piece), :]

    def first(d):
        a = lax.rem(s + d, S)
        return normed.at[pl.ds(al(a * piece, piece), piece), :], a

    for d in range(S):
        src, a = first(d)
        post(src, xst.at[s], xsend.at[d], xsr.at[s], a, r)

    def wfirst(d):
        a = lax.rem(s + d, S)
        head = pl.ds(al(((2 * a * hq) // group) * HEAD, HEAD), HEAD)
        return a, (
            (wq_ref.at[:, pl.ds(al(2 * a * qw, 128), 2 * qw)], wsq.at[s]),
            (wk_ref.at[:, head], wsk.at[s]),
            (wv_ref.at[:, head], wsv.at[s]),
        )

    for d in range(S):
        a, parts = wfirst(d)
        for k, (src, dst) in enumerate(parts):
            post(src, dst, wss.at[k, d], wsr.at[k, s], a, r)

    krows = pl.ds(al(r * kb, kb), kb)

    def second_x(t, _):
        j = lax.rem(p + 1 + t, S)
        arrived(xst.at[j], xsr.at[j])
        post(xst.at[j], xrows(r, s), xz.at[j], xrecv.at[r * S + s], s, 2 * j + c)
        return 0

    lax.fori_loop(0, S, second_x, 0)

    def second_w(t, _):
        j = lax.rem(p + 1 + t, S)
        for k, buf in enumerate((wsq, wsk, wsv)):
            arrived(buf.at[j], wsr.at[k, j])
        for k in range(2):
            post(
                wsq.at[j, :, k * qw : (k + 1) * qw], wqb.at[krows, :],
                wqsend.at[2 * j + k], wqrecv.at[r], s, 2 * j + k,
            )
            post(
                (wsk, wsv)[k].at[j], wkvb.at[krows, :],
                wvsend.at[2 * j + k], wvrecv.at[r], s, 2 * j + k,
            )
        return 0

    lax.fori_loop(0, S, second_w, 0)

    sib = 2 * p + 1 - c

    def relay(j, _):
        seq = 2 * j + c
        ref = xrows(seq, s)
        sem = xrecv.at[seq * S + s]
        arrived(ref, sem)
        for d in range(1, S):
            post(ref, ref, fsend.at[j * S + d - 1], sem, lax.rem(s + d, S), r)
        post(ref, ref, fsend.at[j * S + S - 1], sem, s, sib)
        return 0

    lax.fori_loop(0, S, relay, 0)

    def relay2(j, _):
        seq = 2 * j + c
        for d in range(1, S):
            a = lax.rem(s + d, S)
            ref = xrows(seq, a)
            sem = xrecv.at[seq * S + a]
            arrived(ref, sem)
            post(ref, ref, gsend.at[j * S + d - 1], sem, s, sib)
        return 0

    relay2(0, 0)

    def gather_w(b, _):
        rows = pl.ds(al(b * kb, kb), kb)
        arrived(wqb.at[rows, :], wqrecv.at[b])
        arrived(wkvb.at[rows, :], wvrecv.at[b])
        return 0

    lax.fori_loop(0, n, gather_w, 0)

    is_k = c == 0

    def kvrows(slot, i):
        return kvbuf.at[slot, pl.ds(al(i * R, R), R), :]

    def project(t, _):
        j = t // 2
        other = lax.rem(t, 2)
        i = 2 * j + lax.rem(c + other, 2)

        @pl.when(other == 1)
        def _():
            for a in range(S):
                arrived(xrows(i, a), xrecv.at[i * S + a])

        rows = pl.ds(al(i * R, R), R)
        x = xbuf[rows, :]
        co, si = cos_ref[rows, :], sin_ref[rows, :]
        q = jnp.dot(x, wqb[...], preferred_element_type=jnp.float32)
        for h in range(hq):
            qh = q[:, h * HEAD : (h + 1) * HEAD]
            qbuf[h, rows, :] = (qh * co + pltpu.roll(qh, HEAD // 2, 1) * si).astype(jnp.bfloat16)
        kv = jnp.dot(x, wkvb[...], preferred_element_type=jnp.float32)
        turned = kv * co + pltpu.roll(kv, HEAD // 2, 1) * si
        kvbuf[c, rows, :] = jnp.where(is_k, turned, kv).astype(jnp.bfloat16)
        post(kvrows(c, i), kvrows(c, i), kvsend.at[i], kvrecv.at[i], s, sib)
        return 0

    c2 = LOG2E / (HEAD**0.5)

    def oref(i):
        return obuf.at[i]

    ocols = pl.ds(al(v * qw, 128), qw)

    def attend(i, _):
        arrived(kvrows(1 - c, i), kvrecv.at[i])
        rows = pl.ds(al(i * R, R), R)
        for h in range(hq):
            qh = qbuf[h, rows, :]

            def score(t):
                kk = kvbuf[0, pl.ds(al(t * R, R), R), :]
                return lax.dot_general(
                    qh, kk, (((1,), (1,)), ((), ())), preferred_element_type=jnp.float32
                )

            def pass1(t, m):
                sc = score(t)
                sbuf[t] = sc
                return jnp.maximum(m, sc)

            sc = score(i)
            row = lax.broadcasted_iota(jnp.int32, (R, R), 0)
            col = lax.broadcasted_iota(jnp.int32, (R, R), 1)
            sc = jnp.where(col <= row, sc, -jnp.inf)
            sbuf[i] = sc
            m = lax.fori_loop(0, i, pass1, sc)
            top = jnp.max(m, axis=1, keepdims=True)

            def pass2(t, carry):
                acc, tot = carry
                e = jnp.exp2((sbuf[t] - top) * c2)
                vv = kvbuf[1, pl.ds(al(t * R, R), R), :]
                acc = acc + jnp.dot(
                    e.astype(jnp.bfloat16), vv, preferred_element_type=jnp.float32
                )
                return acc, tot + e

            acc, tot = lax.fori_loop(
                0, i + 1, pass2,
                (jnp.zeros((R, HEAD), jnp.float32), jnp.zeros((R, R), jnp.float32)),
            )
            total = jnp.sum(tot, axis=1, keepdims=True)
            obuf[i, :, h * HEAD : (h + 1) * HEAD] = (acc / total).astype(jnp.bfloat16)
        post(oref(i), out_ref.at[:, ocols], osend.at[i], orecv.at[v], nxt, i)
        return 0

    def stage(j, _):
        lax.fori_loop(jnp.maximum(j, 1), j + 1, relay2, 0)
        lax.fori_loop(2 * j, 2 * j + 2, project, 0)
        lax.fori_loop(2 * j, 2 * j + 2, attend, 0)
        return 0

    lax.fori_loop(0, S, stage, 0)

    for d in range(S):
        src, a = first(d)
        sent(src, xsend.at[d], a, r)
        a, parts = wfirst(d)
        for k, (_, dst) in enumerate(parts):
            sent(dst, wss.at[k, d], a, r)

    def drain(j, _):
        sent(xst.at[j], xz.at[j], s, 2 * j + c)
        for k in range(2):
            sent(wqb.at[krows, :], wqsend.at[2 * j + k], s, 2 * j + k)
            sent(wkvb.at[krows, :], wvsend.at[2 * j + k], s, 2 * j + k)
        ref = xrows(2 * j + c, s)
        for d in range(S):
            pltpu.make_async_copy(ref, ref, fsend.at[j * S + d]).wait()
        for d in range(1, S):
            o = xrows(2 * j + c, lax.rem(s + d, S))
            pltpu.make_async_copy(o, o, gsend.at[j * S + d - 1]).wait()
        return 0

    lax.fori_loop(0, S, drain, 0)

    def drain_out(i, _):
        pltpu.make_async_copy(kvrows(c, i), kvrows(c, i), kvsend.at[i]).wait()
        sent(oref(i), osend.at[i], nxt, i)
        o = out_ref.at[:, pl.ds(al(i * qw, 128), qw)]
        arrived(o, orecv.at[i])
        return 0

    lax.fori_loop(0, n, drain_out, 0)


def per_device(S, n, tokens, norm_gain, w_query, w_key, w_value):
    R, K = tokens.shape[1:]
    T = R * n
    heads = w_query.shape[2] // HEAD
    hq = heads // n
    group = heads // (w_key.shape[2] // HEAD)
    half = HEAD // 2
    freqs = jnp.power(
        jnp.float32(500000.0), -(jnp.arange(half).astype(jnp.float32) * 2.0 / HEAD)
    )
    angles = jnp.arange(T).astype(jnp.float32)[:, None] * freqs[None, :]
    cosine, sine = jnp.cos(angles), jnp.sin(angles)
    co = jnp.concatenate([cosine, cosine], axis=1)
    si = jnp.concatenate([-sine, sine], axis=1)
    vm = pl.BlockSpec(memory_space=pltpu.VMEM)
    hbm = pl.BlockSpec(memory_space=pl.ANY)
    dma = pltpu.SemaphoreType.DMA
    bf = jnp.bfloat16
    out = pl.pallas_call(
        functools.partial(kernel, S, n, hq, group),
        out_shape=jax.ShapeDtypeStruct((R, heads * HEAD), bf),
        in_specs=[vm, vm, hbm, hbm, hbm, vm, vm],
        out_specs=hbm,
        scratch_shapes=[
            pltpu.VMEM((R, K), bf),
            pltpu.VMEM((T, K), bf),
            pltpu.VMEM((K, hq * HEAD), bf),
            pltpu.VMEM((K, HEAD), bf),
            pltpu.VMEM((hq, T, HEAD), bf),
            pltpu.VMEM((2, T, HEAD), bf),
            pltpu.VMEM((n, R, R), jnp.float32),
            pltpu.VMEM((n, R, hq * HEAD), bf),
            pltpu.VMEM((S, R // S, K), bf),
            pltpu.VMEM((S, K // n, 2 * hq * HEAD), bf),
            pltpu.VMEM((S, K // n, HEAD), bf),
            pltpu.VMEM((S, K // n, HEAD), bf),
            dma((S,)), dma((3, S)), dma((3, S)), dma((S,)),
            dma((n * S,)), dma((S,)), dma((S * S,)), dma((S * S,)),
            dma((n,)), dma((n,)), dma((n,)), dma((n,)),
            dma((n,)), dma((n,)), dma((n,)), dma((n,)),
        ],
        compiler_params=pltpu.CompilerParams(
            collective_id=0, has_side_effects=True, vmem_limit_bytes=60 * 1024 * 1024
        ),
    )(tokens[0], norm_gain, w_query[0], w_key[0], w_value[0], co, si)
    return out[None]


def solution(mesh):
    S, n = mesh.shape["section"], mesh.shape["seq"]
    spec = P("section", "seq", None)
    return jax.shard_map(
        functools.partial(per_device, S, n),
        mesh=mesh,
        in_specs=(spec, P("section", None), spec, spec, spec),
        out_specs=spec,
        check_vma=False,
    )
```

```python
import functools

import jax
import jax.numpy as jnp
from jax import lax
from jax.experimental import pallas as pl
from jax.experimental.pallas import tpu as pltpu
from jax.sharding import PartitionSpec as P

HEAD = 128
LOG2E = 1.4426950408889634


def kernel(
    S, n, hq, group,
    tok_ref, gain_ref, wq_ref, wk_ref, wv_ref, cos_ref, sin_ref, out_ref,
    normed, xbuf, wqb, wkvb, qbuf, kvbuf, sbuf, obuf, xst, wsq, wsk, wsv,
    xsr, wsr, wss, xz, xrecv, xsend, fsend, gsend, wqrecv, wqsend, wvrecv, wvsend, kvrecv, kvsend, orecv, osend,
):
    s = lax.axis_index("section")
    r = lax.axis_index("seq")
    p, c = r // 2, lax.rem(r, 2)
    v = 2 * s + c
    R = tok_ref.shape[0]
    T = xbuf.shape[0]
    K = xbuf.shape[1]
    piece = R // S
    kb = wq_ref.shape[0]
    qw = hq * HEAD
    prev = lax.rem(s + S - 1, S)
    nxt = lax.rem(p + 1, S)

    def dev(a, b):
        return {"section": a, "seq": b}

    def al(x, m):
        return pl.multiple_of(x, m)

    def post(src, dst, ssem, rsem, a, b):
        is_self = jnp.logical_and(a == s, b == r)

        @pl.when(is_self)
        def _():
            pltpu.make_async_copy(src, dst, rsem).start()

        @pl.when(jnp.logical_not(is_self))
        def _():
            pltpu.make_async_remote_copy(
                src_ref=src, dst_ref=dst, send_sem=ssem, recv_sem=rsem,
                device_id=dev(a, b), device_id_type=pl.DeviceIdType.MESH,
            ).start()

    def sent(src, ssem, a, b):
        @pl.when(jnp.logical_not(jnp.logical_and(a == s, b == r)))
        def _():
            pltpu.make_async_copy(src, src, ssem).wait()

    def arrived(ref, sem):
        pltpu.make_async_copy(ref, ref, sem).wait()

    barrier = pltpu.get_barrier_semaphore()

    def greet(a, b):
        pl.semaphore_signal(
            barrier, inc=1, device_id=dev(a, b), device_id_type=pl.DeviceIdType.MESH
        )

    for b in range(n):
        greet(s, jnp.int32(b))
    for a in range(S):
        for k in range(2):
            greet(jnp.int32(a), 2 * prev + k)
    for d in range(S):
        greet(lax.rem(s + d, S), r)

    gain = gain_ref[...].astype(jnp.float32)

    def norm_step(i, _):
        rows = pl.ds(al(i * 32, 32), 32)
        wide = tok_ref[rows, :].astype(jnp.float32)
        scale = lax.rsqrt(jnp.mean(wide * wide, axis=-1, keepdims=True) + 1e-05)
        normed[rows, :] = (wide * scale * gain).astype(jnp.bfloat16)
        return 0

    lax.fori_loop(0, R // 32, norm_step, 0)
    pl.semaphore_wait(barrier, 2 * n + S)

    def xrows(seq, a):
        return xbuf.at[pl.ds(al(seq * R + a * piece, piece), piece), :]

    def first(d):
        a = lax.rem(s + d, S)
        return normed.at[pl.ds(al(a * piece, piece), piece), :], a

    for d in range(S):
        src, a = first(d)
        post(src, xst.at[s], xsend.at[d], xsr.at[s], a, r)

    def wfirst(d):
        a = lax.rem(s + d, S)
        head = pl.ds(al(((2 * a * hq) // group) * HEAD, HEAD), HEAD)
        return a, (
            (wq_ref.at[:, pl.ds(al(2 * a * qw, 128), 2 * qw)], wsq.at[s]),
            (wk_ref.at[:, head], wsk.at[s]),
            (wv_ref.at[:, head], wsv.at[s]),
        )

    for d in range(S):
        a, parts = wfirst(d)
        for k, (src, dst) in enumerate(parts):
            post(src, dst, wss.at[k, d], wsr.at[k, s], a, r)

    krows = pl.ds(al(r * kb, kb), kb)

    def second_x(t, _):
        j = lax.rem(p + 1 + t, S)
        arrived(xst.at[j], xsr.at[j])
        post(xst.at[j], xrows(r, s), xz.at[j], xrecv.at[r * S + s], s, 2 * j + c)
        return 0

    lax.fori_loop(0, S, second_x, 0)

    def second_w(t, _):
        j = lax.rem(p + 1 + t, S)
        for k, buf in enumerate((wsq, wsk, wsv)):
            arrived(buf.at[j], wsr.at[k, j])
        for k in range(2):
            post(
                wsq.at[j, :, k * qw : (k + 1) * qw], wqb.at[krows, :],
                wqsend.at[2 * j + k], wqrecv.at[r], s, 2 * j + k,
            )
            post(
                (wsk, wsv)[k].at[j], wkvb.at[krows, :],
                wvsend.at[2 * j + k], wvrecv.at[r], s, 2 * j + k,
            )
        return 0

    sib = 2 * p + 1 - c

    def relay(j, _):
        seq = 2 * j + c
        ref = xrows(seq, s)
        sem = xrecv.at[seq * S + s]
        arrived(ref, sem)
        for d in range(1, S):
            post(ref, ref, fsend.at[j * S + d - 1], sem, lax.rem(s + d, S), r)
        post(ref, ref, fsend.at[j * S + S - 1], sem, s, sib)
        return 0

    def hops(t, _):
        relay(t, 0)
        second_w(t, 0)
        return 0

    lax.fori_loop(0, S, hops, 0)

    def relay2(j, _):
        seq = 2 * j + c
        for d in range(1, S):
            a = lax.rem(s + d, S)
            ref = xrows(seq, a)
            sem = xrecv.at[seq * S + a]
            arrived(ref, sem)
            post(ref, ref, gsend.at[j * S + d - 1], sem, s, sib)
        return 0

    relay2(0, 0)

    def gather_w(b, _):
        rows = pl.ds(al(b * kb, kb), kb)
        arrived(wqb.at[rows, :], wqrecv.at[b])
        arrived(wkvb.at[rows, :], wvrecv.at[b])
        return 0

    lax.fori_loop(0, n, gather_w, 0)

    is_k = c == 0

    def kvrows(slot, i):
        return kvbuf.at[slot, pl.ds(al(i * R, R), R), :]

    def project(t, _):
        j = t // 2
        other = lax.rem(t, 2)
        i = 2 * j + lax.rem(c + other, 2)

        @pl.when(other == 1)
        def _():
            for a in range(S):
                arrived(xrows(i, a), xrecv.at[i * S + a])

        rows = pl.ds(al(i * R, R), R)
        x = xbuf[rows, :]
        co, si = cos_ref[rows, :], sin_ref[rows, :]
        q = jnp.dot(x, wqb[...], preferred_element_type=jnp.float32)
        for h in range(hq):
            qh = q[:, h * HEAD : (h + 1) * HEAD]
            qbuf[h, rows, :] = (qh * co + pltpu.roll(qh, HEAD // 2, 1) * si).astype(jnp.bfloat16)
        kv = jnp.dot(x, wkvb[...], preferred_element_type=jnp.float32)
        turned = kv * co + pltpu.roll(kv, HEAD // 2, 1) * si
        kvbuf[c, rows, :] = jnp.where(is_k, turned, kv).astype(jnp.bfloat16)
        post(kvrows(c, i), kvrows(c, i), kvsend.at[i], kvrecv.at[i], s, sib)
        return 0

    c2 = LOG2E / (HEAD**0.5)

    def oref(i):
        return obuf.at[i]

    ocols = pl.ds(al(v * qw, 128), qw)

    def attend(i, _):
        arrived(kvrows(1 - c, i), kvrecv.at[i])
        rows = pl.ds(al(i * R, R), R)
        for h in range(hq):
            qh = qbuf[h, rows, :]

            def score(t):
                kk = kvbuf[0, pl.ds(al(t * R, R), R), :]
                return lax.dot_general(
                    qh, kk, (((1,), (1,)), ((), ())), preferred_element_type=jnp.float32
                )

            def pass1(t, m):
                sc = score(t)
                sbuf[t] = sc
                return jnp.maximum(m, sc)

            sc = score(i)
            row = lax.broadcasted_iota(jnp.int32, (R, R), 0)
            col = lax.broadcasted_iota(jnp.int32, (R, R), 1)
            sc = jnp.where(col <= row, sc, -jnp.inf)
            sbuf[i] = sc
            m = lax.fori_loop(0, i, pass1, sc)
            top = jnp.max(m, axis=1, keepdims=True)

            def pass2(t, carry):
                acc, tot = carry
                e = jnp.exp2((sbuf[t] - top) * c2)
                vv = kvbuf[1, pl.ds(al(t * R, R), R), :]
                acc = acc + jnp.dot(
                    e.astype(jnp.bfloat16), vv, preferred_element_type=jnp.float32
                )
                return acc, tot + e

            acc, tot = lax.fori_loop(
                0, i + 1, pass2,
                (jnp.zeros((R, HEAD), jnp.float32), jnp.zeros((R, R), jnp.float32)),
            )
            total = jnp.sum(tot, axis=1, keepdims=True)
            obuf[i, :, h * HEAD : (h + 1) * HEAD] = (acc / total).astype(jnp.bfloat16)
        post(oref(i), out_ref.at[:, ocols], osend.at[i], orecv.at[v], nxt, i)
        return 0

    def stage(j, _):
        lax.fori_loop(jnp.maximum(j, 1), j + 1, relay2, 0)
        lax.fori_loop(2 * j, 2 * j + 2, project, 0)
        lax.fori_loop(2 * j, 2 * j + 2, attend, 0)
        return 0

    lax.fori_loop(0, S, stage, 0)

    for d in range(S):
        src, a = first(d)
        sent(src, xsend.at[d], a, r)
        a, parts = wfirst(d)
        for k, (_, dst) in enumerate(parts):
            sent(dst, wss.at[k, d], a, r)

    def drain(j, _):
        sent(xst.at[j], xz.at[j], s, 2 * j + c)
        for k in range(2):
            sent(wqb.at[krows, :], wqsend.at[2 * j + k], s, 2 * j + k)
            sent(wkvb.at[krows, :], wvsend.at[2 * j + k], s, 2 * j + k)
        ref = xrows(2 * j + c, s)
        for d in range(S):
            pltpu.make_async_copy(ref, ref, fsend.at[j * S + d]).wait()
        for d in range(1, S):
            o = xrows(2 * j + c, lax.rem(s + d, S))
            pltpu.make_async_copy(o, o, gsend.at[j * S + d - 1]).wait()
        return 0

    lax.fori_loop(0, S, drain, 0)

    def drain_out(i, _):
        pltpu.make_async_copy(kvrows(c, i), kvrows(c, i), kvsend.at[i]).wait()
        sent(oref(i), osend.at[i], nxt, i)
        o = out_ref.at[:, pl.ds(al(i * qw, 128), qw)]
        arrived(o, orecv.at[i])
        return 0

    lax.fori_loop(0, n, drain_out, 0)


def per_device(S, n, tokens, norm_gain, w_query, w_key, w_value):
    R, K = tokens.shape[1:]
    T = R * n
    heads = w_query.shape[2] // HEAD
    hq = heads // n
    group = heads // (w_key.shape[2] // HEAD)
    half = HEAD // 2
    freqs = jnp.power(
        jnp.float32(500000.0), -(jnp.arange(half).astype(jnp.float32) * 2.0 / HEAD)
    )
    angles = jnp.arange(T).astype(jnp.float32)[:, None] * freqs[None, :]
    cosine, sine = jnp.cos(angles), jnp.sin(angles)
    co = jnp.concatenate([cosine, cosine], axis=1)
    si = jnp.concatenate([-sine, sine], axis=1)
    vm = pl.BlockSpec(memory_space=pltpu.VMEM)
    hbm = pl.BlockSpec(memory_space=pl.ANY)
    dma = pltpu.SemaphoreType.DMA
    bf = jnp.bfloat16
    out = pl.pallas_call(
        functools.partial(kernel, S, n, hq, group),
        out_shape=jax.ShapeDtypeStruct((R, heads * HEAD), bf),
        in_specs=[vm, vm, hbm, hbm, hbm, vm, vm],
        out_specs=hbm,
        scratch_shapes=[
            pltpu.VMEM((R, K), bf),
            pltpu.VMEM((T, K), bf),
            pltpu.VMEM((K, hq * HEAD), bf),
            pltpu.VMEM((K, HEAD), bf),
            pltpu.VMEM((hq, T, HEAD), bf),
            pltpu.VMEM((2, T, HEAD), bf),
            pltpu.VMEM((n, R, R), jnp.float32),
            pltpu.VMEM((n, R, hq * HEAD), bf),
            pltpu.VMEM((S, R // S, K), bf),
            pltpu.VMEM((S, K // n, 2 * hq * HEAD), bf),
            pltpu.VMEM((S, K // n, HEAD), bf),
            pltpu.VMEM((S, K // n, HEAD), bf),
            dma((S,)), dma((3, S)), dma((3, S)), dma((S,)),
            dma((n * S,)), dma((S,)), dma((S * S,)), dma((S * S,)),
            dma((n,)), dma((n,)), dma((n,)), dma((n,)),
            dma((n,)), dma((n,)), dma((n,)), dma((n,)),
        ],
        compiler_params=pltpu.CompilerParams(
            collective_id=0, has_side_effects=True, vmem_limit_bytes=60 * 1024 * 1024
        ),
    )(tokens[0], norm_gain, w_query[0], w_key[0], w_value[0], co, si)
    return out[None]


def solution(mesh):
    S, n = mesh.shape["section"], mesh.shape["seq"]
    spec = P("section", "seq", None)
    return jax.shard_map(
        functools.partial(per_device, S, n),
        mesh=mesh,
        in_specs=(spec, P("section", None), spec, spec, spec),
        out_specs=spec,
        check_vma=False,
    )
```

```python
import functools

import jax
import jax.numpy as jnp
from jax import lax
from jax.experimental import pallas as pl
from jax.experimental.pallas import tpu as pltpu
from jax.sharding import PartitionSpec as P

HEAD = 128
LOG2E = 1.4426950408889634


def kernel(
    S, n, hq, group,
    tok_ref, gain_ref, wq_ref, wk_ref, wv_ref, cos_ref, sin_ref, out_ref,
    normed, xbuf, wqb, wkvb, qbuf, kvbuf, sbuf, obuf, xst, wsq, wsk, wsv,
    xsr, wsr, wss, xz, xrecv, xsend, fsend, gsend, wqrecv, wqsend, wvrecv, wvsend, kvrecv, kvsend, orecv, osend,
):
    s = lax.axis_index("section")
    r = lax.axis_index("seq")
    p, c = r // 2, lax.rem(r, 2)
    v = 2 * s + c
    R = tok_ref.shape[0]
    T = xbuf.shape[0]
    K = xbuf.shape[1]
    piece = R // S
    kb = wq_ref.shape[0]
    qw = hq * HEAD
    prev = lax.rem(s + S - 1, S)
    nxt = lax.rem(p + 1, S)

    def dev(a, b):
        return {"section": a, "seq": b}

    def al(x, m):
        return pl.multiple_of(x, m)

    def post(src, dst, ssem, rsem, a, b):
        is_self = jnp.logical_and(a == s, b == r)

        @pl.when(is_self)
        def _():
            pltpu.make_async_copy(src, dst, rsem).start()

        @pl.when(jnp.logical_not(is_self))
        def _():
            pltpu.make_async_remote_copy(
                src_ref=src, dst_ref=dst, send_sem=ssem, recv_sem=rsem,
                device_id=dev(a, b), device_id_type=pl.DeviceIdType.MESH,
            ).start()

    def sent(src, ssem, a, b):
        @pl.when(jnp.logical_not(jnp.logical_and(a == s, b == r)))
        def _():
            pltpu.make_async_copy(src, src, ssem).wait()

    def arrived(ref, sem):
        pltpu.make_async_copy(ref, ref, sem).wait()

    barrier = pltpu.get_barrier_semaphore()

    def greet(a, b):
        pl.semaphore_signal(
            barrier, inc=1, device_id=dev(a, b), device_id_type=pl.DeviceIdType.MESH
        )

    for b in range(n):
        greet(s, jnp.int32(b))
    for a in range(S):
        for k in range(2):
            greet(jnp.int32(a), 2 * prev + k)
    for d in range(S):
        greet(lax.rem(s + d, S), r)

    gain = gain_ref[...].astype(jnp.float32)

    def norm_step(i, _):
        rows = pl.ds(al(i * 32, 32), 32)
        wide = tok_ref[rows, :].astype(jnp.float32)
        scale = lax.rsqrt(jnp.mean(wide * wide, axis=-1, keepdims=True) + 1e-05)
        normed[rows, :] = (wide * scale * gain).astype(jnp.bfloat16)
        return 0

    lax.fori_loop(0, R // 32, norm_step, 0)
    pl.semaphore_wait(barrier, 2 * n + S)

    def xrows(seq, a):
        return xbuf.at[pl.ds(al(seq * R + a * piece, piece), piece), :]

    def first(d):
        a = lax.rem(s + d, S)
        return normed.at[pl.ds(al(a * piece, piece), piece), :], a

    for d in range(S):
        src, a = first(d)
        post(src, xst.at[s], xsend.at[d], xsr.at[s], a, r)

    def wfirst(d):
        a = lax.rem(s + d, S)
        head = pl.ds(al(((2 * a * hq) // group) * HEAD, HEAD), HEAD)
        return a, (
            (wq_ref.at[:, pl.ds(al(2 * a * qw, 128), 2 * qw)], wsq.at[s]),
            (wk_ref.at[:, head], wsk.at[s]),
            (wv_ref.at[:, head], wsv.at[s]),
        )

    for d in range(S):
        a, parts = wfirst(d)
        for k, (src, dst) in enumerate(parts):
            post(src, dst, wss.at[k, d], wsr.at[k, s], a, r)

    krows = pl.ds(al(r * kb, kb), kb)

    def second_x(t, _):
        j = lax.rem(p + 1 + t, S)
        arrived(xst.at[j], xsr.at[j])
        post(xst.at[j], xrows(r, s), xz.at[j], xrecv.at[r * S + s], s, 2 * j + c)
        return 0

    lax.fori_loop(0, S, second_x, 0)

    def second_w(t, _):
        j = lax.rem(p + 1 + t, S)
        for k, buf in enumerate((wsq, wsk, wsv)):
            arrived(buf.at[j], wsr.at[k, j])
        for k in range(2):
            post(
                wsq.at[j, :, k * qw : (k + 1) * qw], wqb.at[krows, :],
                wqsend.at[2 * j + k], wqrecv.at[r], s, 2 * j + k,
            )
            post(
                (wsk, wsv)[k].at[j], wkvb.at[krows, :],
                wvsend.at[2 * j + k], wvrecv.at[r], s, 2 * j + k,
            )
        return 0

    lax.fori_loop(0, S, second_w, 0)

    sib = 2 * p + 1 - c

    def relay(j, _):
        seq = 2 * j + c
        ref = xrows(seq, s)
        sem = xrecv.at[seq * S + s]
        arrived(ref, sem)
        for d in range(1, S):
            post(ref, ref, fsend.at[j * S + d - 1], sem, lax.rem(s + d, S), r)
        post(ref, ref, fsend.at[j * S + S - 1], sem, s, sib)
        return 0

    lax.fori_loop(0, S, relay, 0)

    def relay2(j, _):
        seq = 2 * j + c
        for d in range(1, S):
            a = lax.rem(s + d, S)
            ref = xrows(seq, a)
            sem = xrecv.at[seq * S + a]
            arrived(ref, sem)
            post(ref, ref, gsend.at[j * S + d - 1], sem, s, sib)
        return 0

    relay2(0, 0)

    def gather_w(b, _):
        rows = pl.ds(al(b * kb, kb), kb)
        arrived(wqb.at[rows, :], wqrecv.at[b])
        arrived(wkvb.at[rows, :], wvrecv.at[b])
        return 0

    lax.fori_loop(0, n, gather_w, 0)

    is_k = c == 0

    def kvrows(slot, i):
        return kvbuf.at[slot, pl.ds(al(i * R, R), R), :]

    def project(t, _):
        j = t // 2
        other = lax.rem(t, 2)
        i = 2 * j + lax.rem(c + other, 2)

        @pl.when(other == 1)
        def _():
            for a in range(S):
                arrived(xrows(i, a), xrecv.at[i * S + a])

        rows = pl.ds(al(i * R, R), R)
        x = xbuf[rows, :]
        co, si = cos_ref[rows, :], sin_ref[rows, :]
        q = jnp.dot(x, wqb[...], preferred_element_type=jnp.float32)
        for h in range(hq):
            qh = q[:, h * HEAD : (h + 1) * HEAD]
            qbuf[h, rows, :] = (qh * co + pltpu.roll(qh, HEAD // 2, 1) * si).astype(jnp.bfloat16)
        kv = jnp.dot(x, wkvb[...], preferred_element_type=jnp.float32)
        turned = kv * co + pltpu.roll(kv, HEAD // 2, 1) * si
        kvbuf[c, rows, :] = jnp.where(is_k, turned, kv).astype(jnp.bfloat16)
        post(kvrows(c, i), kvrows(c, i), kvsend.at[i], kvrecv.at[i], s, sib)
        return 0

    c2 = LOG2E / (HEAD**0.5)

    def oref(i):
        return obuf.at[i]

    ocols = pl.ds(al(v * qw, 128), qw)

    def attend(i, _):
        arrived(kvrows(1 - c, i), kvrecv.at[i])
        rows = pl.ds(al(i * R, R), R)
        heads = range(hq)

        def fold(op, x):
            parts = [x[:, k : k + HEAD] for k in range(0, R, HEAD)]
            return functools.reduce(op, parts)

        def score(h, t):
            return lax.dot_general(
                qbuf[h, rows, :], kvbuf[0, pl.ds(al(t * R, R), R), :],
                (((1,), (1,)), ((), ())), preferred_element_type=jnp.float32,
            )

        def pass1(t, ms):
            scs = [score(h, t) for h in heads]
            for h in heads:
                sbuf[h, t] = scs[h]
            return tuple(jnp.maximum(ms[h], fold(jnp.maximum, scs[h])) for h in heads)

        row = lax.broadcasted_iota(jnp.int32, (R, R), 0)
        col = lax.broadcasted_iota(jnp.int32, (R, R), 1)
        first_max = []
        for h in heads:
            sc = jnp.where(col <= row, score(h, i), -jnp.inf)
            sbuf[h, i] = sc
            first_max.append(fold(jnp.maximum, sc))
        ms = lax.fori_loop(0, i, pass1, tuple(first_max))
        tops = [jnp.max(m, axis=1, keepdims=True) for m in ms]

        def pass2(t, carry):
            vv = kvbuf[1, pl.ds(al(t * R, R), R), :]
            new = []
            for h in heads:
                acc, tot = carry[h]
                e = jnp.exp2((sbuf[h, t] - tops[h]) * c2)
                acc = acc + jnp.dot(
                    e.astype(jnp.bfloat16), vv, preferred_element_type=jnp.float32
                )
                new.append((acc, tot + fold(jnp.add, e)))
            return tuple(new)

        zero = jnp.zeros((R, HEAD), jnp.float32)
        sums = lax.fori_loop(0, i + 1, pass2, tuple((zero, zero) for _ in heads))
        for h in heads:
            acc, tot = sums[h]
            total = jnp.sum(tot, axis=1, keepdims=True)
            obuf[i, :, h * HEAD : (h + 1) * HEAD] = (acc / total).astype(jnp.bfloat16)
        post(oref(i), out_ref.at[:, ocols], osend.at[i], orecv.at[v], nxt, i)
        return 0

    def stage(j, _):
        lax.fori_loop(jnp.maximum(j, 1), j + 1, relay2, 0)
        lax.fori_loop(2 * j, 2 * j + 2, project, 0)
        lax.fori_loop(2 * j, 2 * j + 2, attend, 0)
        return 0

    lax.fori_loop(0, S, stage, 0)

    for d in range(S):
        src, a = first(d)
        sent(src, xsend.at[d], a, r)
        a, parts = wfirst(d)
        for k, (_, dst) in enumerate(parts):
            sent(dst, wss.at[k, d], a, r)

    def drain(j, _):
        sent(xst.at[j], xz.at[j], s, 2 * j + c)
        for k in range(2):
            sent(wqb.at[krows, :], wqsend.at[2 * j + k], s, 2 * j + k)
            sent(wkvb.at[krows, :], wvsend.at[2 * j + k], s, 2 * j + k)
        ref = xrows(2 * j + c, s)
        for d in range(S):
            pltpu.make_async_copy(ref, ref, fsend.at[j * S + d]).wait()
        for d in range(1, S):
            o = xrows(2 * j + c, lax.rem(s + d, S))
            pltpu.make_async_copy(o, o, gsend.at[j * S + d - 1]).wait()
        return 0

    lax.fori_loop(0, S, drain, 0)

    def drain_out(i, _):
        pltpu.make_async_copy(kvrows(c, i), kvrows(c, i), kvsend.at[i]).wait()
        sent(oref(i), osend.at[i], nxt, i)
        o = out_ref.at[:, pl.ds(al(i * qw, 128), qw)]
        arrived(o, orecv.at[i])
        return 0

    lax.fori_loop(0, n, drain_out, 0)


def per_device(S, n, tokens, norm_gain, w_query, w_key, w_value):
    R, K = tokens.shape[1:]
    T = R * n
    heads = w_query.shape[2] // HEAD
    hq = heads // n
    group = heads // (w_key.shape[2] // HEAD)
    half = HEAD // 2
    freqs = jnp.power(
        jnp.float32(500000.0), -(jnp.arange(half).astype(jnp.float32) * 2.0 / HEAD)
    )
    angles = jnp.arange(T).astype(jnp.float32)[:, None] * freqs[None, :]
    cosine, sine = jnp.cos(angles), jnp.sin(angles)
    co = jnp.concatenate([cosine, cosine], axis=1)
    si = jnp.concatenate([-sine, sine], axis=1)
    vm = pl.BlockSpec(memory_space=pltpu.VMEM)
    hbm = pl.BlockSpec(memory_space=pl.ANY)
    dma = pltpu.SemaphoreType.DMA
    bf = jnp.bfloat16
    out = pl.pallas_call(
        functools.partial(kernel, S, n, hq, group),
        out_shape=jax.ShapeDtypeStruct((R, heads * HEAD), bf),
        in_specs=[vm, vm, hbm, hbm, hbm, vm, vm],
        out_specs=hbm,
        scratch_shapes=[
            pltpu.VMEM((R, K), bf),
            pltpu.VMEM((T, K), bf),
            pltpu.VMEM((K, hq * HEAD), bf),
            pltpu.VMEM((K, HEAD), bf),
            pltpu.VMEM((hq, T, HEAD), bf),
            pltpu.VMEM((2, T, HEAD), bf),
            pltpu.VMEM((hq, n, R, R), jnp.float32),
            pltpu.VMEM((n, R, hq * HEAD), bf),
            pltpu.VMEM((S, R // S, K), bf),
            pltpu.VMEM((S, K // n, 2 * hq * HEAD), bf),
            pltpu.VMEM((S, K // n, HEAD), bf),
            pltpu.VMEM((S, K // n, HEAD), bf),
            dma((S,)), dma((3, S)), dma((3, S)), dma((S,)),
            dma((n * S,)), dma((S,)), dma((S * S,)), dma((S * S,)),
            dma((n,)), dma((n,)), dma((n,)), dma((n,)),
            dma((n,)), dma((n,)), dma((n,)), dma((n,)),
        ],
        compiler_params=pltpu.CompilerParams(
            collective_id=0, has_side_effects=True, vmem_limit_bytes=60 * 1024 * 1024
        ),
    )(tokens[0], norm_gain, w_query[0], w_key[0], w_value[0], co, si)
    return out[None]


def solution(mesh):
    S, n = mesh.shape["section"], mesh.shape["seq"]
    spec = P("section", "seq", None)
    return jax.shard_map(
        functools.partial(per_device, S, n),
        mesh=mesh,
        in_specs=(spec, P("section", None), spec, spec, spec),
        out_specs=spec,
        check_vma=False,
    )
```
